512 devices in a mesh: chain: 64 (over y, z_lo, x), tp: 8 (over z_hi, core).
Axes of the slice: x: 4, y: 8, z: 8 (z_hi: 4, z_lo: 2; z = z_hi * 2 + z_lo), core: 2. Of those that a mesh axis runs over, the one named last changes fastest.
Arguments:
- hidden: bfloat16 [8192, 5120], P('chain', 'tp'), may hold values from -1000 to 1000
- segments: int32 [8192], P('chain'), may hold values from 0 to 255, never falling along the last dimension, each value on 1 to 128 neighbouring positions
- in_gain: float32 [5120], replicated, may hold values from 0.1 to 1.9
- q_gain: float32 [128], replicated, may hold values from 0.5 to 2.5
- k_gain: float32 [128], replicated, may hold values from 0.5 to 2.5
- w_query: bfloat16 [5120, 4096], P('chain', 'tp'), may hold values from -0.078125 to 0.078125
- w_key: bfloat16 [5120, 1024], P('chain', 'tp'), may hold values from -0.078125 to 0.078125
- w_value: bfloat16 [5120, 1024], P('chain', 'tp'), may hold values from -0.078125 to 0.078125
Outputs:
- context: bfloat16 [8192, 4096], P('chain', 'tp')
The draws below stay inside these ranges and needn't reach their ends.
Inputs may be any that keep to these rules, and one draw needn't show every extreme that they name: `segments`: document ids never fall along the tokens; a document holds at most 128 tokens and some document holds exactly 128.
All inputs are finite; a program needn't handle non-finite values.
Results may differ from the reference program's by a relative error of at most 0.0085.
Values may be sent and summed in bfloat16 or wider, within the bound.
A program may use at most 64 MiB of HBM per device.

```python
import math
import jax
import jax.numpy as jnp
import numpy as np
from jax import lax

D = 5120
HEAD = 128
QH = 32
KVH = 8
TOK = 128
TOKENS = 8192
QW = 4096
KW = 1024
N_CHAIN = 64


def draw_hidden(key, part):
    key = jax.random.fold_in(key, 11)
    first, second, third = jax.random.split(key, 3)
    columns = jnp.exp(jax.random.uniform(third, (1, D), jnp.float32, 0.0, math.log(10.0)))
    rows = jnp.exp(jax.random.uniform(second, (TOKENS, 1), jnp.float32, 0.0, math.log(10.0)))
    values = jnp.clip(jax.random.normal(first, (TOKENS, D), jnp.float32), -6.0, 6.0) * rows * columns
    return values.astype(jnp.bfloat16)


def block_levels(key, extent, cuts, smallest, top_value):
    loudness, own = 1.0, jax.random.fold_in(key, 6)
    for position, parts in cuts:
        steps = jnp.exp(jax.random.uniform(jax.random.fold_in(own, position), (parts,), jnp.float32, smallest / len(cuts), top_value / len(cuts)))
        loudness = loudness * jnp.repeat(steps, extent[position] // parts).reshape([-1 if axis == position else 1 for axis in range(len(extent))])
    return loudness


def split_up(amount, total, reach, lean):
    weights = [(1 << 20) // math.isqrt(rank ** lean) + 1 for rank in range(2, amount + 1)]
    spare, holding = total - reach - (amount - 1), [1] * (amount - 1)
    while spare > 0:
        movable = [i for i in range(amount - 1) if holding[i] < reach]
        whole, left = sum([weights[i] for i in movable]), spare
        for i in movable:
            more = min(reach - holding[i], max(1, left * weights[i] // whole), spare)
            holding[i] = holding[i] + more
            spare = spare - more
    return np.array([reach] + holding)


def uneven_parts(rng, count, total, reach, skew):
    if count == 2:
        one = jax.random.randint(rng, (), max(1, total - reach), min(reach, total - 1) + 1)
        return jnp.stack([one, total - one])
    sizes = jnp.asarray(split_up(count, total, reach, skew), jnp.int32)
    couples = (count - 1) // 2
    source_of, sink = sizes[1:1 + 2 * couples:2], sizes[2:2 + 2 * couples:2]
    room = jnp.minimum(source_of - 1, reach - sink)
    passed = jax.random.randint(jax.random.fold_in(rng, 1), (couples,), 0, 1 << 20) % (room + 1)
    sizes = sizes.at[1:1 + 2 * couples:2].set(source_of - passed).at[2:2 + 2 * couples:2].set(sink + passed)
    return sizes[jax.random.permutation(jax.random.fold_in(rng, 2), count)]


def noise(rng, extent, spread, bound, shards=(), held_as=jnp.bfloat16):
    values = jax.random.normal(rng, extent, jnp.float32) * spread
    if len(shards) > 0:
        values = block_levels(rng, extent, shards, -0.22, 0.18) * values
    return jnp.clip(values, min=-bound, max=bound).astype(held_as)


def setup_inputs(seed: int = 0) -> dict:
    key_of = jax.random.split(jax.random.key(seed), 9)
    hidden = draw_hidden(jax.random.fold_in(key_of[8], 71), 0)
    segments = jnp.searchsorted(jnp.cumsum(uneven_parts(key_of[1], 4 * N_CHAIN, TOKENS, TOK, 2)), jnp.arange(TOKENS), side="right").astype(jnp.int32)
    in_gain = jnp.clip(1.0 + 0.18 * jax.random.normal(key_of[2], (D,), jnp.float32), 0.1, 1.9)
    q_gain = jnp.clip(jnp.exp(jax.random.uniform(key_of[3], (HEAD,), jnp.float32, math.log(0.5), math.log(2.5))), 0.5, 2.5)
    k_gain = jnp.clip(jnp.exp(jax.random.uniform(key_of[4], (HEAD,), jnp.float32, math.log(0.5), math.log(2.5))), 0.5, 2.5)
    w_query = noise(key_of[5], (D, QW), D ** -0.5, 0.078125, ((0, 64), (1, 8)))
    w_key = noise(key_of[6], (D, KW), D ** -0.5, 0.078125, ((0, 64), (1, 8)))
    w_value = noise(key_of[7], (D, KW), D ** -0.5, 0.078125, ((0, 64), (1, 8)))
    return {"hidden": hidden, "segments": segments, "in_gain": in_gain, "q_gain": q_gain, "k_gain": k_gain, "w_query": w_query, "w_key": w_key, "w_value": w_value}


EPSILON = 1e-06
ROPE_BASE = 1000000.0

def root_norm(values, gain):
    return values * lax.rsqrt(lax.optimization_barrier(jnp.mean(values * values, axis=-1, keepdims=True)) + EPSILON) * gain

def positions(segment_ids):
    length = segment_ids.shape[0]
    ordinal = jnp.arange(length, dtype=jnp.int32)
    change = jnp.concatenate([jnp.ones((1,), jnp.int32), (segment_ids[1:] != segment_ids[:-1]).astype(jnp.int32)])
    starts = lax.cummax(ordinal * change, axis=0)
    return (ordinal - starts, ordinal)

def rotate(values, offsets):
    half_dim = values.shape[-1] // 2
    ladder = jnp.arange(half_dim, dtype=jnp.float32)
    frequency = ROPE_BASE ** (-2.0 * ladder / values.shape[-1])
    angles = offsets.astype(jnp.float32)[:, None] * frequency[None, :]
    cosine = jnp.cos(angles)[:, None, :]
    sine = jnp.sin(angles)[:, None, :]
    first = values[..., :half_dim]
    second = values[..., half_dim:]
    return jnp.concatenate([first * cosine - second * sine, second * cosine + first * sine], axis=-1)

def attention(queries, key_rows, value_rows, segment_ids, ordinal):
    length, group, head_dim = queries.shape
    block = min(256, length)
    scale = head_dim ** (-0.5)

    def one_block(start):
        rows = lax.dynamic_slice_in_dim(queries, start, block, 0)
        rows = jnp.transpose(rows, (1, 0, 2)).reshape(group * block, head_dim)
        logits = jnp.dot(rows, key_rows.T, preferred_element_type=jnp.float32) * scale
        query_pos = lax.dynamic_slice_in_dim(ordinal, start, block, 0)
        query_seg = lax.dynamic_slice_in_dim(segment_ids, start, block, 0)
        allowed = (ordinal[None, :] <= query_pos[:, None]) & (segment_ids[None, :] == query_seg[:, None])
        allowed = jnp.tile(allowed, (group, 1))
        expo = jnp.where(allowed, jnp.exp(logits), 0.0)
        attend_weights = (expo / lax.optimization_barrier(jnp.sum(expo, axis=-1, keepdims=True))).astype(jnp.bfloat16)
        context = jnp.dot(attend_weights, value_rows, preferred_element_type=jnp.float32).astype(jnp.bfloat16)
        return jnp.transpose(context.reshape(group, block, head_dim), (1, 0, 2))
    starts = jnp.arange(length // block, dtype=jnp.int32) * block
    blocks = lax.map(one_block, starts)
    return blocks.reshape(length, group, head_dim)

def forward_span(hidden, segment_ids, in_gain, q_gain, k_gain, w_query, w_key, w_value):
    length = hidden.shape[0]
    normed = root_norm(hidden.astype(jnp.float32), in_gain).astype(jnp.bfloat16)
    queries = jnp.dot(normed, w_query, preferred_element_type=jnp.float32)
    key_rows = jnp.dot(normed, w_key, preferred_element_type=jnp.float32)
    value_rows = jnp.dot(normed, w_value, preferred_element_type=jnp.float32)
    offsets, ordinal = positions(segment_ids)
    queries = rotate(root_norm(queries.reshape(length, QH, HEAD), q_gain), offsets).astype(jnp.bfloat16)
    key_rows = rotate(root_norm(key_rows.reshape(length, KVH, HEAD), k_gain), offsets).astype(jnp.bfloat16)
    value_rows = value_rows.astype(jnp.bfloat16).reshape(length, KVH, HEAD)
    group = QH // KVH

    def one_head(kv_head):
        chosen = lax.dynamic_slice_in_dim(queries, kv_head * group, group, 1)
        key_one = lax.dynamic_index_in_dim(key_rows, kv_head, 1, keepdims=False)
        value_one = lax.dynamic_index_in_dim(value_rows, kv_head, 1, keepdims=False)
        return attention(chosen, key_one, value_one, segment_ids, ordinal)
    heads = lax.map(one_head, jnp.arange(KVH, dtype=jnp.int32))
    return jnp.transpose(heads, (1, 0, 2, 3)).reshape(length, QH * HEAD)

def reference(hidden, segments, in_gain, q_gain, k_gain, w_query, w_key, w_value):
    spans = hidden.reshape(N_CHAIN, TOK, D)
    span_ids = segments.reshape(N_CHAIN, TOK)

    def one_span(paired):
        return forward_span(paired[0], paired[1], in_gain, q_gain, k_gain, w_query, w_key, w_value)
    result = lax.map(one_span, (spans, span_ids))
    return result.reshape(TOKENS, QH * HEAD)
```

```python
import jax
import jax.numpy as jnp
from jax import lax
from jax.experimental import pallas as pl
from jax.experimental.pallas import tpu as pltpu
from jax.sharding import PartitionSpec as P

D = 5120
HEAD = 128
TOK = 128
EPSILON = 1e-06
ROPE_BASE = 1000000.0
MESH = pl.DeviceIdType.MESH

NY, NZ, NX, NH, NK = 8, 2, 4, 4, 2
ROWS = 80
PART = NZ * ROWS
DEPTH = NY * PART
CHUNKS = 3
WIDE = 256
LOCAL = D // (NH * NK)
F32 = jnp.float32
BF16 = jnp.bfloat16


def kernel(
    hidden, segments, in_gain, q_gain, k_gain, w_query, w_key, w_value, out,
    hid, in_gain_v, segments_v, q_gain_v, k_gain_v, staged, h_t, h_n, weights, part_send, part_recv, part_own, squares, squares_all, heads,
    load_sem, zx_s, zx_r, y_s, y_r, y4_s, y4_r, xa_s, xa_r, hz_s, hz_r, hc_s, hc_r, sq_s, sq_r, pr_s, pr_r,
):
    chain, tp = lax.axis_index("chain"), lax.axis_index("tp")
    y, z, x = chain // (NZ * NX), (chain // NX) % NZ, chain % NX
    zh, core = tp // NK, tp % NK

    def at(y_=0, z_=0, x_=0, h_=0, k_=0):
        return {
            "chain": ((y + y_) % NY * NZ + (z + z_) % NZ) * NX + (x + x_) % NX,
            "tp": (zh + h_) % NH * NK + (core + k_) % NK,
        }

    def remote(src, dst, send, recv, to):
        return pltpu.make_async_remote_copy(
            src_ref=src, dst_ref=dst, send_sem=send, recv_sem=recv, device_id=to, device_id_type=MESH
        )

    def rows_of(y_):
        return ((y_ % NK) * NH + y_ // NK) * PART

    def block(y_, z_):
        return pl.ds(pl.multiple_of(rows_of(y_) + z_ * ROWS, 16), ROWS)

    mine = block(y, z)
    loads = [
        pltpu.make_async_copy(hidden, hid, load_sem.at[0]),
        pltpu.make_async_copy(w_key, weights.at[0, mine, pl.ds(0, HEAD)], load_sem.at[1]),
        pltpu.make_async_copy(w_value, weights.at[0, mine, pl.ds(HEAD, HEAD)], load_sem.at[2]),
        pltpu.make_async_copy(w_query.at[:, pl.ds(0, WIDE)], weights.at[1, mine], load_sem.at[3]),
        pltpu.make_async_copy(w_query.at[:, pl.ds(WIDE, WIDE)], weights.at[2, mine], load_sem.at[4]),
        pltpu.make_async_copy(in_gain, in_gain_v, load_sem.at[5]),
        pltpu.make_async_copy(segments, segments_v, load_sem.at[6]),
        pltpu.make_async_copy(q_gain, q_gain_v, load_sem.at[7]),
        pltpu.make_async_copy(k_gain, k_gain_v, load_sem.at[8]),
    ]
    for load in loads:
        load.start()

    partners = (
        [at(y_=1), at(y_=-1), at(z_=1), at(k_=1)]
        + [at(x_=i) for i in range(1, NX)]
        + [at(h_=i) for i in range(1, NH)]
    )
    barrier = pltpu.get_barrier_semaphore()
    for partner in partners:
        pl.semaphore_signal(barrier, inc=1, device_id=partner, device_id_type=MESH)

    loads[0].wait()
    loads[5].wait()
    raw = hid[...].astype(F32)
    gain = in_gain_v[0:1, pl.ds(pl.multiple_of(tp * LOCAL, 128), LOCAL)]
    turned = (raw * gain).T.astype(BF16)
    for i in range(NX):
        staged[i, :ROWS] = turned[i * ROWS : (i + 1) * ROWS]
        staged[i, ROWS:] = turned[(NX + i) * ROWS : (NX + i + 1) * ROWS]
    own_rows = pl.ds(pl.multiple_of(rows_of(tp), 16), PART)
    h_t[0, own_rows] = staged[x]
    square = jnp.sum(raw * raw, axis=1, keepdims=True)
    squares[0] = jnp.broadcast_to(square, (TOK, TOK)).T[:8]

    for load in loads[1:5] + loads[6:]:
        load.wait()
    pl.semaphore_wait(barrier, len(partners))

    zx = [
        remote(weights.at[c, mine], weights.at[c, mine], zx_s.at[c], zx_r.at[c], at(z_=1))
        for c in range(CHUNKS)
    ]

    def y_copy(c, step, p, right):
        origin = (y - (step - 1)) % NY if right else (y + (step - 1)) % NY
        region = weights.at[c, block(origin, (z + p) % NZ)]
        i = (c * 3 + step - 1) * 4 + p * 2 + (0 if right else 1)
        return remote(region, region, y_s.at[i], y_r.at[i], at(y_=1 if right else -1))

    def y_last(c, right):
        region = weights.at[c, block((y - 3) % NY, 0) if right else block((y + 3) % NY, 1)]
        i = c * 2 + (0 if right else 1)
        return remote(region, region, y4_s.at[i], y4_r.at[i], at(y_=1 if right else -1))

    def weights_step(c, step, p):
        for right in (True, False):
            if step > 1:
                y_copy(c, step - 1, p, right).wait_recv()
            y_copy(c, step, p, right).start()

    def weights_last(c):
        for p in range(NZ):
            for right in (True, False):
                y_copy(c, 3, p, right).wait_recv()
        for right in (True, False):
            y_last(c, right).start()

    to_x = {1: 1, 2: -1, 3: 2}
    xa = {
        q: remote(staged.at[(x + d) % NX], h_t.at[q, own_rows], xa_s.at[q - 1], xa_r.at[q - 1], at(x_=d))
        for q, d in to_x.items()
    }

    def hz_direct(q, right):
        region = h_t.at[q, own_rows]
        i = q * 4 + (0 if right else 1)
        return remote(region, region, hz_s.at[i], hz_r.at[i], at(h_=1 if right else -1))

    def hz_relay(q, right):
        source = (tp - NK) % (NH * NK) if right else (tp + NK) % (NH * NK)
        start = rows_of(source) + (0 if right else ROWS)
        region = h_t.at[q, pl.ds(pl.multiple_of(start, 16), ROWS)]
        i = q * 4 + (2 if right else 3)
        return remote(region, region, hz_s.at[i], hz_r.at[i], at(h_=1 if right else -1))

    def hz_start(q):
        if q > 0:
            xa[q].wait_recv()
        hz_direct(q, True).start()
        hz_direct(q, False).start()

    def hz_pass(q):
        hz_direct(q, True).wait_recv()
        hz_relay(q, True).start()
        hz_direct(q, False).wait_recv()
        hz_relay(q, False).start()

    half = pl.ds(pl.multiple_of(core * (NH * PART), 16), NH * PART)
    hc = [
        remote(h_t.at[q, half], h_t.at[q, half], hc_s.at[q], hc_r.at[q], at(k_=1)) for q in range(NX)
    ]

    def hc_start(q):
        hz_relay(q, True).wait_recv()
        hz_relay(q, False).wait_recv()
        hc[q].start()

    def turn(q):
        hc[q].wait_recv()
        h_n[pl.ds(q * TOK, TOK)] = h_t[q].T

    sq = [
        remote(squares.at[0], squares.at[i], sq_s.at[i], sq_r.at[i], at(h_=i)) for i in range(1, NH)
    ]
    sq_core = remote(squares_all.at[0], squares_all.at[1], sq_s.at[0], sq_r.at[0], at(k_=1))

    def project(c):
        y_last(c, True).wait_recv()
        y_last(c, False).wait_recv()
        total = jnp.dot(h_n[...], weights[c], preferred_element_type=F32)
        part_own[c] = total[:TOK]
        for q in range(1, NX):
            part_send[c, q - 1] = total[q * TOK : (q + 1) * TOK].astype(BF16)
        for q in (3, 1, 2):
            partial(c, q).start()

    def partial(c, q):
        back = {1: -1, 2: 1, 3: 2}[q]
        i = c * 3 + q - 1
        return remote(part_send.at[c, q - 1], part_recv.at[c, q - 1], pr_s.at[i], pr_r.at[i], at(x_=back))

    for c in range(CHUNKS):
        zx[c].start()
    for c in range(CHUNKS):
        weights_step(c, 1, 0)
    for q in (3, 1, 2):
        xa[q].start()
    hz_start(0)
    for copy in sq:
        copy.start()

    seg = jnp.broadcast_to(segments_v[...].astype(F32), (TOK, TOK))
    query_pos = lax.broadcasted_iota(jnp.int32, (TOK, TOK), 0)
    key_pos = lax.broadcasted_iota(jnp.int32, (TOK, TOK), 1)
    allowed = jnp.where((seg == seg.T) & (key_pos <= query_pos), 1.0, 0.0)
    offset = jnp.sum(allowed, axis=1, keepdims=True) - 1.0
    ladder = (key_pos % (HEAD // 2)).astype(F32)
    frequency = jnp.exp(ladder * (-2.0 / HEAD * 13.815510557964274))
    angle = offset * frequency
    heads[0] = jnp.cos(angle)
    heads[1] = jnp.sin(angle) * jnp.where(key_pos < HEAD // 2, -1.0, 1.0)
    heads[2] = allowed

    zx[0].wait_recv()
    weights_step(0, 1, 1)
    hz_start(1)
    hz_start(2)
    zx[1].wait_recv()
    weights_step(1, 1, 1)
    hz_start(3)
    zx[2].wait_recv()
    weights_step(2, 1, 1)
    for p in range(NZ):
        weights_step(0, 2, p)
    hz_pass(0)
    for p in range(NZ):
        weights_step(1, 2, p)
    hz_pass(1)
    for p in range(NZ):
        weights_step(2, 2, p)
    hz_pass(2)
    for p in range(NZ):
        weights_step(0, 3, p)
    hz_pass(3)
    hc_start(0)
    for p in range(NZ):
        weights_step(1, 3, p)
    hc_start(1)
    turn(0)
    for p in range(NZ):
        weights_step(2, 3, p)
    hc_start(2)
    turn(1)
    weights_last(0)
    hc_start(3)
    turn(2)
    weights_last(1)
    for copy in sq:
        copy.wait_recv()
    squares_all[0] = (squares[0] + squares[1]) + (squares[2] + squares[3])
    sq_core.start()
    turn(3)
    weights_last(2)
    for c in range(CHUNKS):
        project(c)
    sq_core.wait_recv()
    token_squares = jnp.broadcast_to((squares_all[0] + squares_all[1])[:1], (TOK, TOK)).T
    inverse = lax.rsqrt(token_squares / D + EPSILON)

    def gathered(c):
        for q in range(1, NX):
            partial(c, q).wait_recv()
        total = part_own[c]
        for q in range(1, NX):
            total = total + part_recv[c, q - 1].astype(F32)
        return total[:, :HEAD] * inverse, total[:, HEAD:] * inverse

    def rotated(values, gain):
        mean = jnp.mean(values * values, axis=1, keepdims=True)
        normed = values * lax.rsqrt(mean + EPSILON) * gain
        return (normed * heads[0] + pltpu.roll(normed, HEAD // 2, 1) * heads[1]).astype(BF16)

    keys, values = gathered(0)
    keys = rotated(keys, k_gain_v[...])
    values = values.astype(BF16)
    for c in range(1, CHUNKS):
        for i, query in enumerate(gathered(c)):
            query = rotated(query, q_gain_v[...])
            logits = lax.dot_general(query, keys, (((1,), (1,)), ((), ())), preferred_element_type=F32)
            expo = jnp.where(heads[2] > 0.5, jnp.exp(logits * HEAD**-0.5), 0.0)
            attend = (expo / jnp.sum(expo, axis=1, keepdims=True)).astype(BF16)
            context = jnp.dot(attend, values, preferred_element_type=F32).astype(BF16)
            out[:, pl.ds(((c - 1) * 2 + i) * HEAD, HEAD)] = context

    for c in range(CHUNKS):
        zx[c].wait_send()
        for right in (True, False):
            for p in range(NZ):
                for step in (1, 2, 3):
                    y_copy(c, step, p, right).wait_send()
            y_last(c, right).wait_send()
        for q in range(1, NX):
            partial(c, q).wait_send()
    for q in range(NX):
        if q:
            xa[q].wait_send()
        for right in (True, False):
            hz_direct(q, right).wait_send()
            hz_relay(q, right).wait_send()
        hc[q].wait_send()
    for copy in sq:
        copy.wait_send()
    sq_core.wait_send()


def per_device(hidden, segments, in_gain, q_gain, k_gain, w_query, w_key, w_value):
    vmem = pl.BlockSpec(memory_space=pltpu.VMEM)
    hbm = pl.BlockSpec(memory_space=pl.ANY)
    dma = pltpu.SemaphoreType.DMA
    return pl.pallas_call(
        kernel,
        name="layer",
        out_shape=jax.ShapeDtypeStruct((TOK, 4 * HEAD), BF16),
        in_specs=[hbm] * 8,
        out_specs=vmem,
        scratch_shapes=[
            pltpu.VMEM((TOK, LOCAL), BF16),
            pltpu.VMEM((1, D), F32),
            pltpu.VMEM((1, TOK), jnp.int32),
            pltpu.VMEM((1, HEAD), F32),
            pltpu.VMEM((1, HEAD), F32),
            pltpu.VMEM((NX, PART, TOK), BF16),
            pltpu.VMEM((NX, DEPTH, TOK), BF16),
            pltpu.VMEM((NX * TOK, DEPTH), BF16),
            pltpu.VMEM((CHUNKS, DEPTH, WIDE), BF16),
            pltpu.VMEM((CHUNKS, NX - 1, TOK, WIDE), BF16),
            pltpu.VMEM((CHUNKS, NX - 1, TOK, WIDE), BF16),
            pltpu.VMEM((CHUNKS, TOK, WIDE), F32),
            pltpu.VMEM((NH, 8, TOK), F32),
            pltpu.VMEM((2, 8, TOK), F32),
            pltpu.VMEM((3, TOK, TOK), F32),
            dma((9,)),
            dma((CHUNKS,)), dma((CHUNKS,)),
            dma((CHUNKS * 12,)), dma((CHUNKS * 12,)),
            dma((CHUNKS * 2,)), dma((CHUNKS * 2,)),
            dma((NX - 1,)), dma((NX - 1,)),
            dma((NX * 4,)), dma((NX * 4,)),
            dma((NX,)), dma((NX,)),
            dma((NH,)), dma((NH,)),
            dma((CHUNKS * 3,)), dma((CHUNKS * 3,)),
        ],
        compiler_params=pltpu.CompilerParams(
            collective_id=0, has_side_effects=True, vmem_limit_bytes=64 * 2**20
        ),
    )(
        hidden,
        segments.reshape(1, TOK),
        in_gain.reshape(1, D),
        q_gain.reshape(1, HEAD),
        k_gain.reshape(1, HEAD),
        w_query,
        w_key,
        w_value,
    )


def solution(mesh):
    placed = (
        P("chain", "tp"), P("chain"), P(), P(), P(), P("chain", "tp"), P("chain", "tp"), P("chain", "tp"),
    )
    return jax.shard_map(
        per_device, mesh=mesh, in_specs=placed, out_specs=P("chain", "tp"), check_vma=False
    )
```

```python
import jax
import jax.numpy as jnp
from jax import lax
from jax.experimental import pallas as pl
from jax.experimental.pallas import tpu as pltpu
from jax.sharding import PartitionSpec as P

D = 5120
HEAD = 128
TOK = 128
EPSILON = 1e-06
ROPE_BASE = 1000000.0
MESH = pl.DeviceIdType.MESH

NY, NZ, NX, NH, NK = 8, 2, 4, 4, 2
ROWS = 80
PART = NZ * ROWS
DEPTH = NY * PART
CHUNKS = (2, 2, 2)
ROUTES = {(3, True): (0, 0), (1, False): (0, 160), (0, True): (0, 160), (2, False): (0, 0)}
PAIR, STEP, LAST, SWAP, SEND, PASS, CORE, TURN, PROJECT, DONE, SQUARES, SUM, SCALE, TABLES, MEET = range(15)
ORDER_0 = (
    (PAIR, 0), (PAIR, 1), (PAIR, 2), (SWAP, 3), (SWAP, 1), (SWAP, 2), (STEP, 0, 1, 0), (STEP, 1, 1, 0),
    (STEP, 2, 1, 0), (STEP, 0, 1, 1), (STEP, 1, 1, 1), (STEP, 0, 2, 0), (STEP, 2, 1, 1), (STEP, 1, 2, 0), (MEET, 1),
    (SEND, 3, True), (SEND, 1, True), (SEND, 2, True), (STEP, 0, 2, 1), (STEP, 1, 2, 1), (STEP, 2, 2, 0), (MEET, 2),
    (STEP, 2, 2, 1), (MEET, 3), (SEND, 3, False), (SEND, 1, False), (SEND, 2, False), (PASS, 0, False), (SQUARES,),
    (STEP, 0, 3, 0), (TABLES,), (STEP, 0, 3, 1), (PASS, 3, False), (STEP, 1, 3, 0), (STEP, 1, 3, 1),
    (PASS, 0, True), (PASS, 1, False), (STEP, 2, 3, 0), (STEP, 2, 3, 1), (PASS, 3, True), (PASS, 2, False),
    (LAST, 0), (LAST, 1), (PASS, 1, True), (SEND, 0, False), (LAST, 2), (PASS, 2, True), (SUM,), (CORE, 3),
    (SCALE,), (CORE, 0), (TURN, 3), (CORE, 1), (SEND, 0, True), (PROJECT, 0, 3), (TURN, 0), (PROJECT, 1, 3),
    (CORE, 2), (TURN, 1), (PROJECT, 0, 1), (PROJECT, 1, 1), (PROJECT, 2, 3), (TURN, 2), (PROJECT, 0, 2),
    (PROJECT, 1, 2), (PROJECT, 2, 1), (PROJECT, 2, 2), (PROJECT, 0, 0), (PROJECT, 1, 0), (PROJECT, 2, 0), (DONE, 0),
    (DONE, 1), (DONE, 2),
)
ORDER_1 = (
    (PAIR, 0), (PAIR, 1), (PAIR, 2), (SWAP, 3), (SWAP, 1), (SWAP, 2), (STEP, 0, 1, 0), (STEP, 1, 1, 0),
    (STEP, 2, 1, 0), (SEND, 0, False), (STEP, 0, 1, 1), (STEP, 1, 1, 1), (SEND, 3, False), (SEND, 1, False),
    (SEND, 2, False), (STEP, 0, 2, 0), (STEP, 2, 1, 1), (STEP, 1, 2, 0), (MEET, 1), (SEND, 3, True),
    (SEND, 1, True), (SEND, 2, True), (STEP, 0, 2, 1), (MEET, 2), (SQUARES,), (STEP, 1, 2, 1), (PASS, 3, True),
    (STEP, 2, 2, 0), (STEP, 2, 2, 1), (PASS, 1, True), (TABLES,), (PASS, 0, False), (STEP, 0, 3, 0),
    (STEP, 0, 3, 1), (PASS, 3, False), (PASS, 2, True), (STEP, 1, 3, 0), (STEP, 1, 3, 1), (PASS, 1, False),
    (SEND, 0, True), (STEP, 2, 3, 0), (STEP, 2, 3, 1), (PASS, 2, False), (LAST, 0), (SUM,), (LAST, 1), (SCALE,),
    (LAST, 2), (CORE, 3), (TURN, 3), (CORE, 1), (PROJECT, 0, 3), (PROJECT, 1, 3), (PROJECT, 2, 3), (TURN, 1),
    (CORE, 2), (PROJECT, 0, 1), (PROJECT, 1, 1), (PROJECT, 2, 1), (TURN, 2), (PASS, 0, True), (CORE, 0),
    (PROJECT, 0, 2), (PROJECT, 1, 2), (PROJECT, 2, 2), (TURN, 0), (PROJECT, 0, 0), (PROJECT, 1, 0), (PROJECT, 2, 0),
    (DONE, 0), (DONE, 1), (DONE, 2),
)
ORDER_2 = (
    (PAIR, 0), (SWAP, 3), (SWAP, 1), (SWAP, 2), (PAIR, 1), (STEP, 0, 1, 0), (PAIR, 2), (STEP, 1, 1, 0),
    (STEP, 2, 1, 0), (SEND, 0, False), (STEP, 0, 1, 1), (SEND, 3, False), (STEP, 1, 1, 1), (SEND, 1, False),
    (SEND, 2, False), (MEET, 1), (SEND, 3, True), (SEND, 1, True), (SEND, 2, True), (SQUARES,), (STEP, 2, 1, 1),
    (STEP, 0, 2, 0), (STEP, 1, 2, 0), (STEP, 0, 2, 1), (STEP, 1, 2, 1), (PASS, 3, True), (PASS, 0, False),
    (STEP, 2, 2, 0), (STEP, 2, 2, 1), (PASS, 1, True), (TABLES,), (PASS, 3, False), (STEP, 0, 3, 0),
    (SEND, 0, True), (STEP, 0, 3, 1), (PASS, 2, True), (PASS, 1, False), (STEP, 1, 3, 0), (STEP, 1, 3, 1),
    (PASS, 2, False), (STEP, 2, 3, 0), (CORE, 3), (STEP, 2, 3, 1), (CORE, 1), (LAST, 0), (TURN, 3), (CORE, 2),
    (PASS, 0, True), (SUM,), (TURN, 1), (LAST, 1), (TURN, 2), (SCALE,), (LAST, 2), (PROJECT, 0, 3), (PROJECT, 0, 1),
    (PROJECT, 0, 2), (PROJECT, 1, 3), (PROJECT, 1, 1), (PROJECT, 1, 2), (PROJECT, 2, 3), (PROJECT, 2, 1),
    (PROJECT, 2, 2), (CORE, 0), (TURN, 0), (PROJECT, 0, 0), (PROJECT, 1, 0), (PROJECT, 2, 0), (DONE, 0), (DONE, 1),
    (DONE, 2),
)
ORDER_3 = (
    (PAIR, 0), (SWAP, 3), (SWAP, 1), (SWAP, 2), (PAIR, 1), (SQUARES,), (PAIR, 2), (STEP, 0, 1, 0), (STEP, 1, 1, 0),
    (SEND, 0, True), (SEND, 0, False), (STEP, 2, 1, 0), (STEP, 0, 1, 1), (SEND, 3, True), (SEND, 3, False),
    (SEND, 1, True), (SEND, 1, False), (SEND, 2, True), (SEND, 2, False), (STEP, 1, 1, 1), (STEP, 2, 1, 1),
    (STEP, 0, 2, 0), (STEP, 1, 2, 0), (STEP, 0, 2, 1), (PASS, 3, False), (PASS, 3, True), (STEP, 1, 2, 1),
    (STEP, 2, 2, 0), (PASS, 1, False), (PASS, 1, True), (TABLES,), (STEP, 2, 2, 1), (STEP, 0, 3, 0),
    (PASS, 2, False), (PASS, 2, True), (STEP, 0, 3, 1), (STEP, 1, 3, 0), (SUM,), (CORE, 3), (STEP, 1, 3, 1),
    (CORE, 1), (STEP, 2, 3, 0), (SCALE,), (TURN, 3), (PASS, 0, True), (STEP, 2, 3, 1), (TURN, 1), (CORE, 2),
    (LAST, 0), (PASS, 0, False), (LAST, 1), (TURN, 2), (CORE, 0), (LAST, 2), (PROJECT, 0, 3), (TURN, 0),
    (PROJECT, 0, 1), (PROJECT, 0, 2), (PROJECT, 1, 3), (PROJECT, 1, 1), (PROJECT, 1, 2), (PROJECT, 2, 3),
    (PROJECT, 2, 1), (PROJECT, 2, 2), (PROJECT, 0, 0), (PROJECT, 1, 0), (PROJECT, 2, 0), (DONE, 0), (DONE, 1),
    (DONE, 2),
)
ORDERS = (ORDER_0, ORDER_1, ORDER_2, ORDER_3)
LOCAL = D // (NH * NK)
F32 = jnp.float32
BF16 = jnp.bfloat16


def kernel(*refs):
    hidden, segments, in_gain, q_gain, k_gain, w_query, w_key, w_value, out = refs[:9]
    hid, in_gain_v, segments_v, q_gain_v, k_gain_v, staged, h_t, h_n, squares, squares_all, heads = refs[9:20]
    load_sem, zx_s, zx_r, y_s, y_r, y4_s, y4_r, xa_s, xa_r, hz_s, hz_r, hc_s, hc_r, sq_s, sq_r, pr_s, pr_r, ready = refs[20:38]
    count = len(CHUNKS)
    weights, part_send, part_recv, part_own = (refs[38 + i * count : 38 + (i + 1) * count] for i in range(4))
    chain, tp = lax.axis_index("chain"), lax.axis_index("tp")
    y, z, x = chain // (NZ * NX), (chain // NX) % NZ, chain % NX
    zh, core = tp // NK, tp % NK

    def at(y_=0, z_=0, x_=0, h_=0, k_=0):
        return {
            "chain": ((y + y_) % NY * NZ + (z + z_) % NZ) * NX + (x + x_) % NX,
            "tp": (zh + h_) % NH * NK + (core + k_) % NK,
        }

    def remote(src, dst, send, recv, to):
        return pltpu.make_async_remote_copy(
            src_ref=src, dst_ref=dst, send_sem=send, recv_sem=recv, device_id=to, device_id_type=MESH
        )

    def rows_of(y_):
        return ((y_ % NK) * NH + y_ // NK) * PART

    def block(y_, z_):
        return pl.ds(pl.multiple_of(rows_of(y_) + z_ * ROWS, 16), ROWS)

    state, swapped = {}, set()
    partners = (
        [at(y_=1), at(y_=-1), at(z_=1), at(k_=1)] + [at(x_=i) for i in range(1, NX)]
    )
    barrier = pltpu.get_barrier_semaphore()
    for partner in partners:
        pl.semaphore_signal(barrier, inc=1, device_id=partner, device_id_type=MESH)
    for i in range(1, NH):

        @pl.when(zh + i < NH)
        def _():
            pl.semaphore_signal(barrier, inc=1, device_id=at(h_=i), device_id_type=MESH)


    mine = block(y, z)
    loads = [
        pltpu.make_async_copy(hidden, hid, load_sem.at[0]),
        pltpu.make_async_copy(in_gain, in_gain_v, load_sem.at[1]),
        pltpu.make_async_copy(segments, segments_v, load_sem.at[2]),
        pltpu.make_async_copy(q_gain, q_gain_v, load_sem.at[3]),
        pltpu.make_async_copy(k_gain, k_gain_v, load_sem.at[4]),
    ]
    columns = [w_key, w_value] + [w_query.at[:, pl.ds(i * HEAD, HEAD)] for i in range(4)]
    place = [(c, i) for c, wide in enumerate(CHUNKS) for i in range(wide)]
    for i, (source, (c, j)) in enumerate(zip(columns, place)):
        target = weights[c].at[mine, pl.ds(j * HEAD, HEAD)]
        loads.append(pltpu.make_async_copy(source, target, load_sem.at[5 + i]))
    for load in loads:
        load.start()

    loads[0].wait()
    loads[1].wait()
    raw = hid[...].astype(F32)
    gain = in_gain_v[0:1, pl.ds(pl.multiple_of(tp * LOCAL, 128), LOCAL)]
    turned = (raw * gain).T.astype(BF16)
    for i in range(NX):
        staged[i, :ROWS] = turned[i * ROWS : (i + 1) * ROWS]
        staged[i, ROWS:] = turned[(NX + i) * ROWS : (NX + i + 1) * ROWS]
    own_rows = pl.ds(pl.multiple_of(rows_of(tp), 16), PART)
    h_t[0, own_rows] = staged[x]
    square = jnp.sum(raw * raw, axis=1, keepdims=True)
    squares[0] = jnp.broadcast_to(square, (TOK, TOK)).T[:8]

    for load in loads[2:]:
        load.wait()
    pl.semaphore_wait(barrier, len(partners) + zh)
    for i in range(1, NH):

        @pl.when(zh >= i)
        def _():
            pl.semaphore_signal(ready.at[i], inc=1, device_id=at(h_=-i), device_id_type=MESH)


    zx = [
        remote(weights[c].at[mine], weights[c].at[mine], zx_s.at[c], zx_r.at[c], at(z_=1))
        for c in range(count)
    ]

    def y_copy(c, step, p, right):
        origin = (y - (step - 1)) % NY if right else (y + (step - 1)) % NY
        region = weights[c].at[block(origin, (z + p) % NZ)]
        i = (c * 3 + step - 1) * 4 + p * 2 + (0 if right else 1)
        return remote(region, region, y_s.at[i], y_r.at[i], at(y_=1 if right else -1))

    def y_last(c, right):
        region = weights[c].at[block((y - 3) % NY, 0) if right else block((y + 3) % NY, 1)]
        i = c * 2 + (0 if right else 1)
        return remote(region, region, y4_s.at[i], y4_r.at[i], at(y_=1 if right else -1))

    def weights_step(c, step, p):
        for right in (True, False):
            if step > 1:
                y_copy(c, step - 1, p, right).wait_recv()
            y_copy(c, step, p, right).start()

    def weights_last(c):
        for p in range(NZ):
            for right in (True, False):
                y_copy(c, 3, p, right).wait_recv()
        for right in (True, False):
            y_last(c, right).start()

    to_x = {1: 1, 2: -1, 3: 2}
    xa = {
        q: remote(staged.at[(x + d) % NX], h_t.at[q, own_rows], xa_s.at[q - 1], xa_r.at[q - 1], at(x_=d))
        for q, d in to_x.items()
    }

    def hz_direct(q, right):
        region = h_t.at[q, own_rows]
        i = q * 4 + (0 if right else 1)
        return remote(region, region, hz_s.at[i], hz_r.at[i], at(h_=1 if right else -1))

    def route(here, right):
        return ROUTES.get((here, right), (0, ROWS) if right else (ROWS, ROWS))

    def hz_relay(q, right, here):
        first, amount = route(here, right)
        source = (tp - NK) % (NH * NK) if right else (tp + NK) % (NH * NK)
        region = h_t.at[q, pl.ds(pl.multiple_of(rows_of(source) + first, 16), amount)]
        i = q * 4 + (2 if right else 3)
        return remote(region, region, hz_s.at[i], hz_r.at[i], at(h_=1 if right else -1))

    def hz_arriving(q, right, here):
        first, amount = route((here - 1) % NH if right else (here + 1) % NH, right)
        if amount:
            source = (tp - 2 * NK) % (NH * NK)
            region = h_t.at[q, pl.ds(pl.multiple_of(rows_of(source) + first, 16), amount)]
            i = q * 4 + (2 if right else 3)
            remote(region, region, hz_s.at[i], hz_r.at[i], at(h_=1 if right else -1)).wait_recv()

    def hz_start(q, right):
        if q > 0 and q not in swapped:
            swapped.add(q)
            xa[q].wait_recv()
        hz_direct(q, right).start()

    def hz_pass(q, right):
        hz_direct(q, right).wait_recv()
        if route(state["here"], right)[1]:
            hz_relay(q, right, state["here"]).start()

    def meet(i):
        pl.semaphore_wait(ready.at[i], 1)

    half = pl.ds(pl.multiple_of(core * (NH * PART), 16), NH * PART)
    hc = [
        remote(h_t.at[q, half], h_t.at[q, half], hc_s.at[q], hc_r.at[q], at(k_=1)) for q in range(NX)
    ]

    def hc_start(q):
        for right in (True, False):
            hz_arriving(q, right, state["here"])
        hc[q].start()

    def turn(q):
        hc[q].wait_recv()
        h_n[pl.ds(q * TOK, TOK)] = h_t[q].T

    sq = [
        remote(squares.at[0], squares.at[i], sq_s.at[i], sq_r.at[i], at(h_=i)) for i in range(1, NH)
    ]
    sq_core = remote(squares_all.at[0], squares_all.at[1], sq_s.at[0], sq_r.at[0], at(k_=1))

    def arrived(c):
        y_last(c, True).wait_recv()
        y_last(c, False).wait_recv()

    def project(c, first, last):
        total = jnp.dot(h_n[pl.ds(first * TOK, (last - first) * TOK)], weights[c][...], preferred_element_type=F32)
        for q in range(first, last):
            piece = total[(q - first) * TOK : (q - first + 1) * TOK]
            if q == 0:
                part_own[c][...] = piece
            else:
                part_send[c][q - 1] = piece.astype(BF16)
        for q in range(last - 1, max(first, 1) - 1, -1):
            partial(c, q).start()

    def partial(c, q):
        back = {1: -1, 2: 1, 3: 2}[q]
        i = c * 3 + q - 1
        return remote(part_send[c].at[q - 1], part_recv[c].at[q - 1], pr_s.at[i], pr_r.at[i], at(x_=back))

    def add_squares():
        for copy in sq:
            copy.wait_recv()
        squares_all[0] = (squares[0] + squares[1]) + (squares[2] + squares[3])
        sq_core.start()

    def scale_squares():
        sq_core.wait_recv()
        token_squares = jnp.broadcast_to((squares_all[0] + squares_all[1])[:1], (TOK, TOK)).T
        heads[3] = lax.rsqrt(token_squares / D + EPSILON)

    def rotated(values, gain):
        mean = jnp.mean(values * values, axis=1, keepdims=True)
        normed = values * lax.rsqrt(mean + EPSILON) * gain
        return (normed * heads[0] + pltpu.roll(normed, HEAD // 2, 1) * heads[1]).astype(BF16)

    key_value = {}

    def finish(c):
        for q in range(1, NX):
            partial(c, q).wait_recv()
        total = part_own[c][...]
        for q in range(1, NX):
            total = total + part_recv[c][q - 1].astype(F32)
        for i, place_ in enumerate(place):
            if place_[0] != c:
                continue
            columns_ = total[:, place_[1] * HEAD : (place_[1] + 1) * HEAD] * heads[3]
            if i == 0:
                key_value[0] = rotated(columns_, k_gain_v[...])
            elif i == 1:
                key_value[1] = columns_.astype(BF16)
            else:
                attention(i - 2, rotated(columns_, q_gain_v[...]))

    def attention(head, query):
        logits = lax.dot_general(query, key_value[0], (((1,), (1,)), ((), ())), preferred_element_type=F32)
        expo = jnp.where(heads[2] > 0.5, jnp.exp(logits * HEAD**-0.5), 0.0)
        attend = (expo / jnp.sum(expo, axis=1, keepdims=True)).astype(BF16)
        context = jnp.dot(attend, key_value[1], preferred_element_type=F32).astype(BF16)
        out[:, pl.ds(head * HEAD, HEAD)] = context

    def tables():
        seg = jnp.broadcast_to(segments_v[...].astype(F32), (TOK, TOK))
        query_pos = lax.broadcasted_iota(jnp.int32, (TOK, TOK), 0)
        key_pos = lax.broadcasted_iota(jnp.int32, (TOK, TOK), 1)
        allowed = jnp.where((seg == seg.T) & (key_pos <= query_pos), 1.0, 0.0)
        offset = jnp.sum(allowed, axis=1, keepdims=True) - 1.0
        ladder = (key_pos % (HEAD // 2)).astype(F32)
        frequency = jnp.exp(ladder * (-2.0 / HEAD * 13.815510557964274))
        angle = offset * frequency
        heads[0] = jnp.cos(angle)
        heads[1] = jnp.sin(angle) * jnp.where(key_pos < HEAD // 2, -1.0, 1.0)
        heads[2] = allowed

    begun = set()

    def project_part(c, q):
        if c not in begun:
            begun.add(c)
            arrived(c)
        project(c, q, q + 1)

    def start_squares():
        for copy in sq:
            copy.start()

    def weights_step_from(c, step, p):
        if step == 1 and p == 1:
            zx[c].wait_recv()
        weights_step(c, step, p)

    actions = {
        PAIR: lambda c: zx[c].start(),
        STEP: weights_step_from,
        LAST: weights_last,
        SWAP: lambda q: xa[q].start(),
        SEND: hz_start,
        PASS: hz_pass,
        CORE: hc_start,
        TURN: turn,
        MEET: meet,
        PROJECT: project_part,
        DONE: finish,
        SQUARES: start_squares,
        SUM: add_squares,
        SCALE: scale_squares,
        TABLES: tables,
    }
    def left(here):
        for c in range(count):
            zx[c].wait_send()
            for right in (True, False):
                for p in range(NZ):
                    for step in (1, 2, 3):
                        y_copy(c, step, p, right).wait_send()
                y_last(c, right).wait_send()
        for q in range(NX):
            if q:
                xa[q].wait_send()
            for right in (True, False):
                hz_direct(q, right).wait_send()
            hc[q].wait_send()
        for copy in sq:
            copy.wait_send()
        sq_core.wait_send()
        for q in range(NX):
            for right in (True, False):
                if route(here, right)[1]:
                    hz_relay(q, right, here).wait_send()

    def run(here, order):
        state["here"] = here
        begun.clear()
        key_value.clear()
        swapped.clear()
        for name, *numbers in order:
            if (name, *numbers) == (DONE, 0):
                left(here)
            actions[name](*numbers)
        for c in range(count):
            for q in range(1, NX):
                partial(c, q).wait_send()

    for here, order in enumerate(ORDERS):
        pl.when(zh == here)(lambda here=here, order=order: run(here, order))


def per_device(hidden, segments, in_gain, q_gain, k_gain, w_query, w_key, w_value):
    vmem = pl.BlockSpec(memory_space=pltpu.VMEM)
    hbm = pl.BlockSpec(memory_space=pltpu.HBM)
    dma = pltpu.SemaphoreType.DMA
    count, widths = len(CHUNKS), [wide * HEAD for wide in CHUNKS]
    return pl.pallas_call(
        kernel,
        name="layer",
        out_shape=jax.ShapeDtypeStruct((TOK, 4 * HEAD), BF16),
        in_specs=[hbm] * 8,
        out_specs=vmem,
        scratch_shapes=[
            pltpu.VMEM((TOK, LOCAL), BF16),
            pltpu.VMEM((1, D), F32),
            pltpu.VMEM((1, TOK), jnp.int32),
            pltpu.VMEM((1, HEAD), F32),
            pltpu.VMEM((1, HEAD), F32),
            pltpu.VMEM((NX, PART, TOK), BF16),
            pltpu.VMEM((NX, DEPTH, TOK), BF16),
            pltpu.VMEM((NX * TOK, DEPTH), BF16),
            pltpu.VMEM((NH, 8, TOK), F32),
            pltpu.VMEM((2, 8, TOK), F32),
            pltpu.VMEM((4, TOK, TOK), F32),
            dma((11,)),
            dma((count,)), dma((count,)),
            dma((count * 12,)), dma((count * 12,)),
            dma((count * 2,)), dma((count * 2,)),
            dma((NX - 1,)), dma((NX - 1,)),
            dma((NX * 4,)), dma((NX * 4,)),
            dma((NX,)), dma((NX,)),
            dma((NH,)), dma((NH,)),
            dma((count * 3,)), dma((count * 3,)),
            pltpu.SemaphoreType.REGULAR((NH,)),
            *[pltpu.VMEM((DEPTH, wide), BF16) for wide in widths],
            *[pltpu.VMEM((NX - 1, TOK, wide), BF16) for wide in widths],
            *[pltpu.VMEM((NX - 1, TOK, wide), BF16) for wide in widths],
            *[pltpu.VMEM((TOK, wide), F32) for wide in widths],
        ],
        compiler_params=pltpu.CompilerParams(
            collective_id=0, has_side_effects=True, vmem_limit_bytes=64 * 2**20
        ),
    )(
        hidden,
        segments.reshape(1, TOK),
        in_gain.reshape(1, D),
        q_gain.reshape(1, HEAD),
        k_gain.reshape(1, HEAD),
        w_query,
        w_key,
        w_value,
    )


def solution(mesh):
    placed = (
        P("chain", "tp"), P("chain"), P(), P(), P(), P("chain", "tp"), P("chain", "tp"), P("chain", "tp"),
    )
    return jax.shard_map(
        per_device, mesh=mesh, in_specs=placed, out_specs=P("chain", "tp"), check_vma=False
    )
```

```python
import jax
import jax.numpy as jnp
from jax import lax
from jax.experimental import pallas as pl
from jax.experimental.pallas import tpu as pltpu
from jax.sharding import PartitionSpec as P

D = 5120
HEAD = 128
TOK = 128
EPSILON = 1e-06
ROPE_BASE = 1000000.0
MESH = pl.DeviceIdType.MESH

NY, NZ, NX, NH, NK = 8, 2, 4, 4, 2
ROWS = 80
PART = NZ * ROWS
DEPTH = NY * PART
CHUNKS = (2, 2, 2)
ROUTES = {(3, True): (0, 0), (1, False): (0, 160), (0, True): (0, 160), (2, False): (0, 0)}
PAIR, STEP, LAST, SWAP, SEND, PASS, CORE, TURN, PROJECT, DONE, SQUARES, SUM, SCALE, TABLES, MEET = range(15)
ORDER_0 = (
    (PAIR, 0), (PAIR, 1), (PAIR, 2), (SWAP, 3), (SWAP, 1), (SWAP, 2), (STEP, 0, 1, 0), (STEP, 1, 1, 0),
    (STEP, 2, 1, 0), (STEP, 0, 1, 1), (STEP, 1, 1, 1), (STEP, 0, 2, 0), (STEP, 2, 1, 1), (STEP, 1, 2, 0), (MEET, 1),
    (SEND, 3, True), (SEND, 1, True), (SEND, 2, True), (STEP, 0, 2, 1), (STEP, 1, 2, 1), (STEP, 2, 2, 0), (MEET, 2),
    (STEP, 2, 2, 1), (MEET, 3), (SEND, 3, False), (SEND, 1, False), (SEND, 2, False), (PASS, 0, False), (SQUARES,),
    (STEP, 0, 3, 0), (TABLES,), (STEP, 0, 3, 1), (PASS, 3, False), (STEP, 1, 3, 0), (STEP, 1, 3, 1),
    (PASS, 0, True), (PASS, 1, False), (STEP, 2, 3, 0), (STEP, 2, 3, 1), (PASS, 3, True), (PASS, 2, False),
    (LAST, 0), (LAST, 1), (PASS, 1, True), (SEND, 0, False), (LAST, 2), (PASS, 2, True), (CORE, 3), (TURN, 3),
    (CORE, 1), (SEND, 0, True), (PROJECT, 0, 3), (PROJECT, 1, 3), (CORE, 2), (TURN, 1), (PROJECT, 0, 1),
    (PROJECT, 1, 1), (PROJECT, 2, 3), (TURN, 2), (PROJECT, 0, 2), (PROJECT, 1, 2), (PROJECT, 2, 1), (PROJECT, 2, 2),
    (CORE, 0), (SUM,), (TURN, 0), (PROJECT, 0, 0), (PROJECT, 1, 0), (PROJECT, 2, 0), (SCALE,), (DONE, 0), (DONE, 1),
    (DONE, 2),
)
ORDER_1 = (
    (PAIR, 0), (PAIR, 1), (PAIR, 2), (SWAP, 3), (SWAP, 1), (SWAP, 2), (STEP, 0, 1, 0), (STEP, 1, 1, 0),
    (STEP, 2, 1, 0), (SEND, 0, False), (STEP, 0, 1, 1), (STEP, 1, 1, 1), (SEND, 3, False), (SEND, 1, False),
    (SEND, 2, False), (STEP, 0, 2, 0), (STEP, 2, 1, 1), (STEP, 1, 2, 0), (MEET, 1), (SEND, 3, True),
    (SEND, 1, True), (SEND, 2, True), (STEP, 0, 2, 1), (MEET, 2), (SQUARES,), (STEP, 1, 2, 1), (PASS, 3, True),
    (STEP, 2, 2, 0), (STEP, 2, 2, 1), (PASS, 1, True), (TABLES,), (PASS, 0, False), (STEP, 0, 3, 0),
    (STEP, 0, 3, 1), (PASS, 3, False), (PASS, 2, True), (STEP, 1, 3, 0), (STEP, 1, 3, 1), (PASS, 1, False),
    (SEND, 0, True), (STEP, 2, 3, 0), (STEP, 2, 3, 1), (PASS, 2, False), (LAST, 0), (LAST, 1), (LAST, 2), (CORE, 3),
    (TURN, 3), (CORE, 1), (PROJECT, 0, 3), (PROJECT, 1, 3), (PROJECT, 2, 3), (TURN, 1), (CORE, 2), (PROJECT, 0, 1),
    (PROJECT, 1, 1), (PROJECT, 2, 1), (TURN, 2), (PASS, 0, True), (PROJECT, 0, 2), (PROJECT, 1, 2), (PROJECT, 2, 2),
    (CORE, 0), (SUM,), (TURN, 0), (PROJECT, 0, 0), (PROJECT, 1, 0), (PROJECT, 2, 0), (SCALE,), (DONE, 0), (DONE, 1),
    (DONE, 2),
)
ORDER_2 = (
    (PAIR, 0), (SWAP, 3), (SWAP, 1), (SWAP, 2), (PAIR, 1), (STEP, 0, 1, 0), (PAIR, 2), (STEP, 1, 1, 0),
    (STEP, 2, 1, 0), (SEND, 0, False), (STEP, 0, 1, 1), (SEND, 3, False), (STEP, 1, 1, 1), (SEND, 1, False),
    (SEND, 2, False), (MEET, 1), (SEND, 3, True), (SEND, 1, True), (SEND, 2, True), (SQUARES,), (STEP, 2, 1, 1),
    (STEP, 0, 2, 0), (STEP, 1, 2, 0), (STEP, 0, 2, 1), (STEP, 1, 2, 1), (PASS, 3, True), (PASS, 0, False),
    (STEP, 2, 2, 0), (STEP, 2, 2, 1), (PASS, 1, True), (TABLES,), (PASS, 3, False), (STEP, 0, 3, 0),
    (SEND, 0, True), (STEP, 0, 3, 1), (PASS, 2, True), (PASS, 1, False), (STEP, 1, 3, 0), (STEP, 1, 3, 1),
    (PASS, 2, False), (STEP, 2, 3, 0), (CORE, 3), (STEP, 2, 3, 1), (CORE, 1), (LAST, 0), (TURN, 3), (CORE, 2),
    (PASS, 0, True), (TURN, 1), (LAST, 1), (TURN, 2), (LAST, 2), (PROJECT, 0, 3), (PROJECT, 0, 1), (PROJECT, 0, 2),
    (PROJECT, 1, 3), (PROJECT, 1, 1), (PROJECT, 1, 2), (PROJECT, 2, 3), (PROJECT, 2, 1), (PROJECT, 2, 2), (CORE, 0),
    (SUM,), (TURN, 0), (PROJECT, 0, 0), (PROJECT, 1, 0), (PROJECT, 2, 0), (SCALE,), (DONE, 0), (DONE, 1), (DONE, 2),
)
ORDER_3 = (
    (PAIR, 0), (SWAP, 3), (SWAP, 1), (SWAP, 2), (PAIR, 1), (SQUARES,), (PAIR, 2), (STEP, 0, 1, 0), (STEP, 1, 1, 0),
    (SEND, 0, True), (SEND, 0, False), (STEP, 2, 1, 0), (STEP, 0, 1, 1), (SEND, 3, True), (SEND, 3, False),
    (SEND, 1, True), (SEND, 1, False), (SEND, 2, True), (SEND, 2, False), (STEP, 1, 1, 1), (STEP, 2, 1, 1),
    (STEP, 0, 2, 0), (STEP, 1, 2, 0), (STEP, 0, 2, 1), (PASS, 3, False), (PASS, 3, True), (STEP, 1, 2, 1),
    (STEP, 2, 2, 0), (PASS, 1, False), (PASS, 1, True), (TABLES,), (STEP, 2, 2, 1), (STEP, 0, 3, 0),
    (PASS, 2, False), (PASS, 2, True), (STEP, 0, 3, 1), (STEP, 1, 3, 0), (CORE, 3), (STEP, 1, 3, 1), (CORE, 1),
    (STEP, 2, 3, 0), (TURN, 3), (PASS, 0, True), (STEP, 2, 3, 1), (TURN, 1), (CORE, 2), (LAST, 0), (PASS, 0, False),
    (LAST, 1), (TURN, 2), (LAST, 2), (PROJECT, 0, 3), (PROJECT, 0, 1), (PROJECT, 0, 2), (PROJECT, 1, 3),
    (PROJECT, 1, 1), (PROJECT, 1, 2), (PROJECT, 2, 3), (PROJECT, 2, 1), (PROJECT, 2, 2), (CORE, 0), (SUM,),
    (TURN, 0), (PROJECT, 0, 0), (PROJECT, 1, 0), (PROJECT, 2, 0), (SCALE,), (DONE, 0), (DONE, 1), (DONE, 2),
)
ORDERS = (ORDER_0, ORDER_1, ORDER_2, ORDER_3)
LOCAL = D // (NH * NK)
F32 = jnp.float32
BF16 = jnp.bfloat16


def kernel(*refs):
    hidden, segments, in_gain, q_gain, k_gain, w_query, w_key, w_value, out = refs[:9]
    hid, in_gain_v, segments_v, q_gain_v, k_gain_v, staged, h_t, h_n, squares, squares_all, heads = refs[9:20]
    load_sem, zx_s, zx_r, y_s, y_r, y4_s, y4_r, xa_s, xa_r, hz_s, hz_r, hc_s, hc_r, sq_s, sq_r, pr_s, pr_r, ready = refs[20:38]
    count = len(CHUNKS)
    weights, part_send, part_recv, part_own = (refs[38 + i * count : 38 + (i + 1) * count] for i in range(4))
    chain, tp = lax.axis_index("chain"), lax.axis_index("tp")
    y, z, x = chain // (NZ * NX), (chain // NX) % NZ, chain % NX
    zh, core = tp // NK, tp % NK

    def at(y_=0, z_=0, x_=0, h_=0, k_=0):
        return {
            "chain": ((y + y_) % NY * NZ + (z + z_) % NZ) * NX + (x + x_) % NX,
            "tp": (zh + h_) % NH * NK + (core + k_) % NK,
        }

    def remote(src, dst, send, recv, to):
        return pltpu.make_async_remote_copy(
            src_ref=src, dst_ref=dst, send_sem=send, recv_sem=recv, device_id=to, device_id_type=MESH
        )

    def rows_of(y_):
        return ((y_ % NK) * NH + y_ // NK) * PART

    def block(y_, z_):
        return pl.ds(pl.multiple_of(rows_of(y_) + z_ * ROWS, 16), ROWS)

    state, swapped = {}, set()
    partners = (
        [at(y_=1), at(y_=-1), at(z_=1), at(k_=1)] + [at(x_=i) for i in range(1, NX)]
    )
    barrier = pltpu.get_barrier_semaphore()
    for partner in partners:
        pl.semaphore_signal(barrier, inc=1, device_id=partner, device_id_type=MESH)
    for i in range(1, NH):

        @pl.when(zh + i < NH)
        def _():
            pl.semaphore_signal(barrier, inc=1, device_id=at(h_=i), device_id_type=MESH)


    mine = block(y, z)
    loads = [
        pltpu.make_async_copy(hidden, hid, load_sem.at[0]),
        pltpu.make_async_copy(in_gain, in_gain_v, load_sem.at[1]),
        pltpu.make_async_copy(segments, segments_v, load_sem.at[2]),
        pltpu.make_async_copy(q_gain, q_gain_v, load_sem.at[3]),
        pltpu.make_async_copy(k_gain, k_gain_v, load_sem.at[4]),
    ]
    columns = [w_key, w_value] + [w_query.at[:, pl.ds(i * HEAD, HEAD)] for i in range(4)]
    place = [(c, i) for c, wide in enumerate(CHUNKS) for i in range(wide)]
    for i, (source, (c, j)) in enumerate(zip(columns, place)):
        target = weights[c].at[mine, pl.ds(j * HEAD, HEAD)]
        loads.append(pltpu.make_async_copy(source, target, load_sem.at[5 + i]))
    for load in loads:
        load.start()

    loads[0].wait()
    loads[1].wait()
    raw = hid[...].astype(F32)
    gain = in_gain_v[0:1, pl.ds(pl.multiple_of(tp * LOCAL, 128), LOCAL)]
    turned = (raw * gain).T.astype(BF16)
    for i in range(NX):
        staged[i, :ROWS] = turned[i * ROWS : (i + 1) * ROWS]
        staged[i, ROWS:] = turned[(NX + i) * ROWS : (NX + i + 1) * ROWS]
    own_rows = pl.ds(pl.multiple_of(rows_of(tp), 16), PART)
    h_t[0, own_rows] = staged[x]
    square = jnp.sum(raw * raw, axis=1, keepdims=True)
    squares[0] = jnp.broadcast_to(square, (TOK, TOK)).T[:8]

    for load in loads[2:]:
        load.wait()
    pl.semaphore_wait(barrier, len(partners) + zh)
    for i in range(1, NH):

        @pl.when(zh >= i)
        def _():
            pl.semaphore_signal(ready.at[i], inc=1, device_id=at(h_=-i), device_id_type=MESH)


    zx = [
        remote(weights[c].at[mine], weights[c].at[mine], zx_s.at[c], zx_r.at[c], at(z_=1))
        for c in range(count)
    ]

    def y_copy(c, step, p, right):
        origin = (y - (step - 1)) % NY if right else (y + (step - 1)) % NY
        region = weights[c].at[block(origin, (z + p) % NZ)]
        i = (c * 3 + step - 1) * 4 + p * 2 + (0 if right else 1)
        return remote(region, region, y_s.at[i], y_r.at[i], at(y_=1 if right else -1))

    def y_last(c, right):
        region = weights[c].at[block((y - 3) % NY, 0) if right else block((y + 3) % NY, 1)]
        i = c * 2 + (0 if right else 1)
        return remote(region, region, y4_s.at[i], y4_r.at[i], at(y_=1 if right else -1))

    def weights_step(c, step, p):
        for right in (True, False):
            if step > 1:
                y_copy(c, step - 1, p, right).wait_recv()
            y_copy(c, step, p, right).start()

    def weights_last(c):
        for p in range(NZ):
            for right in (True, False):
                y_copy(c, 3, p, right).wait_recv()
        for right in (True, False):
            y_last(c, right).start()

    to_x = {1: 1, 2: -1, 3: 2}
    xa = {
        q: remote(staged.at[(x + d) % NX], h_t.at[q, own_rows], xa_s.at[q - 1], xa_r.at[q - 1], at(x_=d))
        for q, d in to_x.items()
    }

    def hz_direct(q, right):
        region = h_t.at[q, own_rows]
        i = q * 4 + (0 if right else 1)
        return remote(region, region, hz_s.at[i], hz_r.at[i], at(h_=1 if right else -1))

    def route(here, right):
        return ROUTES.get((here, right), (0, ROWS) if right else (ROWS, ROWS))

    def hz_relay(q, right, here):
        first, amount = route(here, right)
        source = (tp - NK) % (NH * NK) if right else (tp + NK) % (NH * NK)
        region = h_t.at[q, pl.ds(pl.multiple_of(rows_of(source) + first, 16), amount)]
        i = q * 4 + (2 if right else 3)
        return remote(region, region, hz_s.at[i], hz_r.at[i], at(h_=1 if right else -1))

    def hz_arriving(q, right, here):
        first, amount = route((here - 1) % NH if right else (here + 1) % NH, right)
        if amount:
            source = (tp - 2 * NK) % (NH * NK)
            region = h_t.at[q, pl.ds(pl.multiple_of(rows_of(source) + first, 16), amount)]
            i = q * 4 + (2 if right else 3)
            remote(region, region, hz_s.at[i], hz_r.at[i], at(h_=1 if right else -1)).wait_recv()

    def hz_start(q, right):
        if q > 0 and q not in swapped:
            swapped.add(q)
            xa[q].wait_recv()
        hz_direct(q, right).start()

    def hz_pass(q, right):
        hz_direct(q, right).wait_recv()
        if route(state["here"], right)[1]:
            hz_relay(q, right, state["here"]).start()

    def meet(i):
        pl.semaphore_wait(ready.at[i], 1)

    half = pl.ds(pl.multiple_of(core * (NH * PART), 16), NH * PART)
    hc = [
        remote(h_t.at[q, half], h_t.at[q, half], hc_s.at[q], hc_r.at[q], at(k_=1)) for q in range(NX)
    ]

    def hc_start(q):
        for right in (True, False):
            hz_arriving(q, right, state["here"])
        hc[q].start()

    def turn(q):
        hc[q].wait_recv()
        h_n[pl.ds(q * TOK, TOK)] = h_t[q].T

    sq = [
        remote(squares.at[0], squares.at[i], sq_s.at[i], sq_r.at[i], at(h_=i)) for i in range(1, NH)
    ]
    sq_core = remote(squares_all.at[0], squares_all.at[1], sq_s.at[0], sq_r.at[0], at(k_=1))

    def arrived(c):
        y_last(c, True).wait_recv()
        y_last(c, False).wait_recv()

    def project(c, first, last):
        total = jnp.dot(h_n[pl.ds(first * TOK, (last - first) * TOK)], weights[c][...], preferred_element_type=F32)
        for q in range(first, last):
            piece = total[(q - first) * TOK : (q - first + 1) * TOK]
            if q == 0:
                part_own[c][...] = piece
            else:
                part_send[c][q - 1] = piece.astype(BF16)
        for q in range(last - 1, max(first, 1) - 1, -1):
            partial(c, q).start()

    def partial(c, q):
        back = {1: -1, 2: 1, 3: 2}[q]
        i = c * 3 + q - 1
        return remote(part_send[c].at[q - 1], part_recv[c].at[q - 1], pr_s.at[i], pr_r.at[i], at(x_=back))

    def add_squares():
        for copy in sq:
            copy.wait_recv()
        squares_all[0] = (squares[0] + squares[1]) + (squares[2] + squares[3])
        sq_core.start()

    def scale_squares():
        sq_core.wait_recv()
        token_squares = jnp.broadcast_to((squares_all[0] + squares_all[1])[:1], (TOK, TOK)).T
        heads[3] = lax.rsqrt(token_squares / D + EPSILON)

    def rotated(values, gain):
        mean = jnp.mean(values * values, axis=1, keepdims=True)
        normed = values * lax.rsqrt(mean + EPSILON) * gain
        return (normed * heads[0] + pltpu.roll(normed, HEAD // 2, 1) * heads[1]).astype(BF16)

    key_value = {}

    def finish(c):
        for q in range(1, NX):
            partial(c, q).wait_recv()
        total = part_own[c][...]
        for q in range(1, NX):
            total = total + part_recv[c][q - 1].astype(F32)
        for i, place_ in enumerate(place):
            if place_[0] != c:
                continue
            columns_ = total[:, place_[1] * HEAD : (place_[1] + 1) * HEAD] * heads[3]
            if i == 0:
                key_value[0] = rotated(columns_, k_gain_v[...])
            elif i == 1:
                key_value[1] = columns_.astype(BF16)
            else:
                attention(i - 2, rotated(columns_, q_gain_v[...]))

    def attention(head, query):
        logits = lax.dot_general(query, key_value[0], (((1,), (1,)), ((), ())), preferred_element_type=F32)
        expo = jnp.where(heads[2] > 0.5, jnp.exp(logits * HEAD**-0.5), 0.0)
        attend = (expo / jnp.sum(expo, axis=1, keepdims=True)).astype(BF16)
        context = jnp.dot(attend, key_value[1], preferred_element_type=F32).astype(BF16)
        out[:, pl.ds(head * HEAD, HEAD)] = context

    def tables():
        seg = jnp.broadcast_to(segments_v[...].astype(F32), (TOK, TOK))
        query_pos = lax.broadcasted_iota(jnp.int32, (TOK, TOK), 0)
        key_pos = lax.broadcasted_iota(jnp.int32, (TOK, TOK), 1)
        allowed = jnp.where((seg == seg.T) & (key_pos <= query_pos), 1.0, 0.0)
        offset = jnp.sum(allowed, axis=1, keepdims=True) - 1.0
        ladder = (key_pos % (HEAD // 2)).astype(F32)
        frequency = jnp.exp(ladder * (-2.0 / HEAD * 13.815510557964274))
        angle = offset * frequency
        heads[0] = jnp.cos(angle)
        heads[1] = jnp.sin(angle) * jnp.where(key_pos < HEAD // 2, -1.0, 1.0)
        heads[2] = allowed

    begun = set()

    def project_part(c, q):
        if c not in begun:
            begun.add(c)
            arrived(c)
        project(c, q, q + 1)

    def start_squares():
        for copy in sq:
            copy.start()

    def weights_step_from(c, step, p):
        if step == 1 and p == 1:
            zx[c].wait_recv()
        weights_step(c, step, p)

    actions = {
        PAIR: lambda c: zx[c].start(),
        STEP: weights_step_from,
        LAST: weights_last,
        SWAP: lambda q: xa[q].start(),
        SEND: hz_start,
        PASS: hz_pass,
        CORE: hc_start,
        TURN: turn,
        MEET: meet,
        PROJECT: project_part,
        DONE: finish,
        SQUARES: start_squares,
        SUM: add_squares,
        SCALE: scale_squares,
        TABLES: tables,
    }
    def left(here):
        for c in range(count):
            zx[c].wait_send()
            for right in (True, False):
                for p in range(NZ):
                    for step in (1, 2, 3):
                        y_copy(c, step, p, right).wait_send()
                y_last(c, right).wait_send()
        for q in range(NX):
            if q:
                xa[q].wait_send()
            for right in (True, False):
                hz_direct(q, right).wait_send()
            hc[q].wait_send()
        for copy in sq:
            copy.wait_send()
        sq_core.wait_send()
        for q in range(NX):
            for right in (True, False):
                if route(here, right)[1]:
                    hz_relay(q, right, here).wait_send()

    def run(here, order):
        state["here"] = here
        begun.clear()
        key_value.clear()
        swapped.clear()
        for name, *numbers in order:
            if (name, *numbers) == (DONE, 0):
                left(here)
            actions[name](*numbers)
        for c in range(count):
            for q in range(1, NX):
                partial(c, q).wait_send()

    for here, order in enumerate(ORDERS):
        pl.when(zh == here)(lambda here=here, order=order: run(here, order))


def per_device(hidden, segments, in_gain, q_gain, k_gain, w_query, w_key, w_value):
    vmem = pl.BlockSpec(memory_space=pltpu.VMEM)
    hbm = pl.BlockSpec(memory_space=pltpu.HBM)
    dma = pltpu.SemaphoreType.DMA
    count, widths = len(CHUNKS), [wide * HEAD for wide in CHUNKS]
    return pl.pallas_call(
        kernel,
        name="layer",
        out_shape=jax.ShapeDtypeStruct((TOK, 4 * HEAD), BF16),
        in_specs=[hbm] * 8,
        out_specs=vmem,
        scratch_shapes=[
            pltpu.VMEM((TOK, LOCAL), BF16),
            pltpu.VMEM((1, D), F32),
            pltpu.VMEM((1, TOK), jnp.int32),
            pltpu.VMEM((1, HEAD), F32),
            pltpu.VMEM((1, HEAD), F32),
            pltpu.VMEM((NX, PART, TOK), BF16),
            pltpu.VMEM((NX, DEPTH, TOK), BF16),
            pltpu.VMEM((NX * TOK, DEPTH), BF16),
            pltpu.VMEM((NH, 8, TOK), F32),
            pltpu.VMEM((2, 8, TOK), F32),
            pltpu.VMEM((4, TOK, TOK), F32),
            dma((11,)),
            dma((count,)), dma((count,)),
            dma((count * 12,)), dma((count * 12,)),
            dma((count * 2,)), dma((count * 2,)),
            dma((NX - 1,)), dma((NX - 1,)),
            dma((NX * 4,)), dma((NX * 4,)),
            dma((NX,)), dma((NX,)),
            dma((NH,)), dma((NH,)),
            dma((count * 3,)), dma((count * 3,)),
            pltpu.SemaphoreType.REGULAR((NH,)),
            *[pltpu.VMEM((DEPTH, wide), BF16) for wide in widths],
            *[pltpu.VMEM((NX - 1, TOK, wide), BF16) for wide in widths],
            *[pltpu.VMEM((NX - 1, TOK, wide), BF16) for wide in widths],
            *[pltpu.VMEM((TOK, wide), F32) for wide in widths],
        ],
        compiler_params=pltpu.CompilerParams(
            collective_id=0, has_side_effects=True, vmem_limit_bytes=64 * 2**20
        ),
    )(
        hidden,
        segments.reshape(1, TOK),
        in_gain.reshape(1, D),
        q_gain.reshape(1, HEAD),
        k_gain.reshape(1, HEAD),
        w_query,
        w_key,
        w_value,
    )


def solution(mesh):
    placed = (
        P("chain", "tp"), P("chain"), P(), P(), P(), P("chain", "tp"), P("chain", "tp"), P("chain", "tp"),
    )
    return jax.shard_map(
        per_device, mesh=mesh, in_specs=placed, out_specs=P("chain", "tp"), check_vma=False
    )
```
